32 devices in a mesh: groups: 1, gx: 8 (over z, y), gy: 4 (over x, core).
Axes of the slice: x: 2, y: 2, z: 4, core: 2. Of those that a mesh axis runs over, the one named last changes fastest.
Arguments:
- grid_input: bfloat16 [32, 64, 2048], P('groups', 'gx', 'gy'), may hold values from -6 to 6
- spectral_weight: bfloat16 [2, 32, 32, 8, 1024], P(None, 'gy', 'gx'), may hold values from -1 to 1
- expand_weight: bfloat16 [32, 128], replicated, may hold values from -1 to 1
- reduce_weight: bfloat16 [128, 32], replicated, may hold values from -0.5 to 0.5
- out_cotangent: bfloat16 [32, 64, 2048], P('groups', 'gx', 'gy'), may hold values from -6 to 6
Outputs:
- layer_output: bfloat16 [32, 64, 2048], P('groups', 'gx', 'gy')
- grad_input: bfloat16 [32, 64, 2048], P('groups', 'gx', 'gy')
- grad_spectral: float32 [2, 32, 32, 8, 1024], P('groups', 'gy', 'gx')
- grad_expand: float32 [32, 128], P('groups')
- grad_reduce: float32 [128, 32], P('groups')
The draws below stay inside these ranges and needn't reach their ends.
All inputs are finite; a program needn't handle non-finite values.
Results may differ from the reference program's by a relative error of at most 0.0059.
Values sent between devices are 32-bit elements; how exact they have to be, the bound alone decides.
A program may use at most 64 MiB of HBM per device.

```python
import math
import jax
import jax.numpy as jnp
from jax import lax

C = 32
MLP = 128
NZ = 64
KX = 32
KY = 32
KZ = 8
NX = 64
NY = 32


def steps_of(own_key, shape, shards, smallest, high):
    loudness, own = 1.0, jax.random.fold_in(own_key, 6)
    for axis_at, blocks in shards:
        draws = jnp.exp(jax.random.uniform(jax.random.fold_in(own, axis_at), (blocks,), jnp.float32, smallest / len(shards), high / len(shards)))
        loudness = loudness * jnp.repeat(draws, shape[axis_at] // blocks).reshape([-1 if axis == axis_at else 1 for axis in range(len(shape))])
    return loudness


def centred(key, shape, spread, bound, cuts=(), kind=jnp.bfloat16):
    values = spread * jax.random.normal(key, shape, jnp.float32)
    if cuts:
        values = values * steps_of(key, shape, cuts, -0.22, 0.18)
    return jnp.clip(values, -bound, bound).astype(kind)


def setup_inputs(seed: int = 0, part: int = 0) -> dict:
    streams_of = jax.random.split(jax.random.key(seed), 6)
    part_splits = jax.random.split(jax.random.fold_in(streams_of[5], part), 6)
    grid_input = centred(part_splits[0], (C, NX, NY * NZ), 1.0, 6.0, ((1, 8), (2, 4)))
    spectral_weight = centred(streams_of[1], (2, KX, KY, KZ, C * C), C ** -0.5, 1.0, ((1, 4), (2, 8)))
    expand_weight = centred(streams_of[2], (C, MLP), C ** -0.5, 1.0)
    reduce_weight = centred(streams_of[3], (MLP, C), MLP ** -0.5, 0.5)
    out_cotangent = centred(part_splits[4], (C, NX, NY * NZ), 1.0, 6.0, ((1, 8), (2, 4)))
    return dict(grid_input=grid_input, spectral_weight=spectral_weight, expand_weight=expand_weight, reduce_weight=reduce_weight, out_cotangent=out_cotangent)


precise = lax.Precision.HIGHEST
root_half = 0.7071067811865476
inverse_root_two_pi = 0.3989422804014327

def signed_modes(count_modes):
    index_range = jnp.arange(count_modes, dtype=jnp.int32)
    return jnp.where(index_range < count_modes // 2, index_range, index_range - count_modes)

def phase_pair(length, frequency, orient):
    places = jnp.arange(length, dtype=jnp.int32)
    windings = places[:, None] * frequency[None, :] % length
    angles = windings.astype(jnp.float32) * (2.0 * math.pi / length)
    return (jnp.cos(angles), orient * jnp.sin(angles))

def back_pair(length, frequency):
    cosine, sine_part = phase_pair(length, frequency, 1.0)
    return (cosine.T, sine_part.T)

def along(values, matrix, position):
    contracted = jnp.tensordot(values, matrix, axes=((position,), (0,)), precision=precise)
    return jnp.moveaxis(contracted, -1, position)

def complex_section(spectrum, matrices, position):
    real_part = spectrum[0]
    imag_part = spectrum[1]
    cosine, sine_part = matrices
    offset_pos = position - 1
    return jnp.stack([along(real_part, cosine, offset_pos) - along(imag_part, sine_part, offset_pos), along(real_part, sine_part, offset_pos) + along(imag_part, cosine, offset_pos)])

def full_modes(grid_field):
    cosine, sine_part = phase_pair(NZ, jnp.arange(KZ, dtype=jnp.int32), -1.0)
    spectrum = jnp.stack([along(grid_field, cosine, 3), along(grid_field, sine_part, 3)])
    spectrum = complex_section(spectrum, phase_pair(NX, signed_modes(KX), -1.0), 2)
    return complex_section(spectrum, phase_pair(NY, signed_modes(KY), -1.0), 3)

def full_cells(spectrum):
    spectrum = complex_section(spectrum, back_pair(NY, signed_modes(KY)), 3)
    spectrum = complex_section(spectrum, back_pair(NX, signed_modes(KX)), 2)
    cosine, sine_part = back_pair(NZ, jnp.arange(KZ, dtype=jnp.int32))
    return along(spectrum[0], cosine, 3) - along(spectrum[1], sine_part, 3)

def mix_modes(spectrum, weights):

    def product_part(spectra_in, weights_in):
        return jnp.einsum('cabk,abkco->oabk', spectra_in, weights_in, precision=precise)
    return jnp.stack([product_part(spectrum[0], weights[0]) - product_part(spectrum[1], weights[1]), product_part(spectrum[1], weights[0]) + product_part(spectrum[0], weights[1])])

def mix_adjoint(back_mixed, weights):

    def product_part(spectra_in, weights_in):
        return jnp.einsum('oabk,abkco->cabk', spectra_in, weights_in, precision=precise)
    return jnp.stack([product_part(back_mixed[0], weights[0]) + product_part(back_mixed[1], weights[1]), product_part(back_mixed[1], weights[0]) - product_part(back_mixed[0], weights[1])])

def weight_grad(spectrum, back_mixed):

    def product_part(spectra_in, backs_in):
        return jnp.einsum('cabk,oabk->abkco', spectra_in, backs_in, precision=precise)
    return jnp.stack([product_part(spectrum[0], back_mixed[0]) + product_part(spectrum[1], back_mixed[1]), product_part(spectrum[0], back_mixed[1]) - product_part(spectrum[1], back_mixed[0])])

def erf_gelu(values):
    return 0.5 * values * (1.0 + lax.erf(values * root_half))

def gelu_slope(values):
    return 0.5 * (1.0 + lax.erf(values * root_half)) + values * jnp.exp(-0.5 * values * values) * inverse_root_two_pi

def pointwise(grid_slab, spectral, expand_weight, reduce_weight, cotangent_slab):
    joined = (spectral + grid_slab.astype(jnp.float32)).astype(jnp.bfloat16)
    before = lax.dot_general(expand_weight, joined, (((0,), (0,)), ((), ())), preferred_element_type=jnp.float32)
    hidden = erf_gelu(before).astype(jnp.bfloat16)
    output = lax.dot_general(reduce_weight, hidden, (((0,), (0,)), ((), ())), preferred_element_type=jnp.float32)
    back_hidden = jnp.dot(reduce_weight, cotangent_slab, preferred_element_type=jnp.float32)
    back_before = (back_hidden * gelu_slope(before)).astype(jnp.bfloat16)
    grad_reduce = lax.dot_general(hidden, cotangent_slab, (((1,), (1,)), ((), ())), preferred_element_type=jnp.float32)
    grad_expand = lax.dot_general(joined, back_before, (((1,), (1,)), ((), ())), preferred_element_type=jnp.float32)
    back_joined = jnp.dot(expand_weight, back_before, preferred_element_type=jnp.float32)
    return (output.astype(jnp.bfloat16), back_joined, grad_expand, grad_reduce)

def reference(grid_input, spectral_weight, expand_weight, reduce_weight, out_cotangent):
    mode_scale = 1.0 / math.sqrt(NX * NY * NZ * KX * KY * (4 * KZ - 3))
    doubling = jnp.where(jnp.arange(KZ) == 0, 1.0, 2.0).astype(jnp.float32) * mode_scale
    spectrum = full_modes(grid_input.astype(jnp.float32).reshape(C, NX, NY, NZ))
    weights = spectral_weight.astype(jnp.float32).reshape(2, KX, KY, KZ, C, C)
    mixed_modes = mix_modes(spectrum, weights) * doubling
    spectral = full_cells(mixed_modes).reshape(C, NX, NY * NZ)

    def slab_step(running, slab_inputs):
        grid_slab, spectral_slab, cotangent_slab = slab_inputs
        output_slab, back_slab, expand_part, reduce_part = pointwise(grid_slab, spectral_slab, expand_weight, reduce_weight, cotangent_slab)
        return ((running[0] + expand_part, running[1] + reduce_part), (output_slab, back_slab))
    initial = (jnp.zeros((C, MLP), jnp.float32), jnp.zeros((MLP, C), jnp.float32))
    totals, stacked = lax.scan(slab_step, initial, (jnp.moveaxis(grid_input, 1, 0), jnp.moveaxis(spectral, 1, 0), jnp.moveaxis(out_cotangent, 1, 0)))
    layer_output = jnp.moveaxis(stacked[0], 0, 1)
    back_joined = jnp.moveaxis(stacked[1], 0, 1)
    rms_scale = 1.0 / math.sqrt(NX * NY * NZ)
    grad_expand = totals[0] * rms_scale
    grad_reduce = totals[1] * rms_scale
    back_mixed = full_modes(back_joined.reshape(C, NX, NY, NZ)) * doubling
    grad_spectral = weight_grad(spectrum, back_mixed).reshape(2, KX, KY, KZ, C * C)
    back_modes = mix_adjoint(back_mixed, weights)
    grad_input = (back_joined + full_cells(back_modes).reshape(C, NX, NY * NZ)).astype(jnp.bfloat16)
    return (layer_output, grad_input, grad_spectral, grad_expand, grad_reduce)
```

```python
import math

import jax
import jax.numpy as jnp
import ml_dtypes
import numpy as np
from jax import lax
from jax.experimental import pallas as pl
from jax.experimental.pallas import tpu as pltpu
from jax.sharding import PartitionSpec as P

NZ = 64
KX = 32
KY = 32
KZ = 8


precise = lax.Precision.HIGHEST
root_half = 0.7071067811865476
inverse_root_two_pi = 0.3989422804014327


def signed_modes(count_modes):
    index_range = jnp.arange(count_modes, dtype=jnp.int32)
    return jnp.where(index_range < count_modes // 2, index_range, index_range - count_modes)


def phase_pair(length, frequency, orient):
    places = jnp.arange(length, dtype=jnp.int32)
    windings = places[:, None] * frequency[None, :] % length
    angles = windings.astype(jnp.float32) * (2.0 * math.pi / length)
    return (jnp.cos(angles), orient * jnp.sin(angles))


def back_pair(length, frequency):
    cosine, sine_part = phase_pair(length, frequency, 1.0)
    return (cosine.T, sine_part.T)


def along(values, matrix, position):
    contracted = jnp.tensordot(values, matrix, axes=((position,), (0,)), precision=precise)
    return jnp.moveaxis(contracted, -1, position)


def complex_section(spectrum, matrices, position):
    real_part = spectrum[0]
    imag_part = spectrum[1]
    cosine, sine_part = matrices
    offset_pos = position - 1
    return jnp.stack(
        [
            along(real_part, cosine, offset_pos) - along(imag_part, sine_part, offset_pos),
            along(real_part, sine_part, offset_pos) + along(imag_part, cosine, offset_pos),
        ]
    )


def to_modes(grid_field, width_x, width_y):
    cosine, sine_part = phase_pair(NZ, jnp.arange(KZ, dtype=jnp.int32), -1.0)
    spectrum = jnp.stack([along(grid_field, cosine, 3), along(grid_field, sine_part, 3)])
    forward_x = phase_pair(width_x, signed_modes(KX), -1.0)
    forward_y = phase_pair(width_y, signed_modes(KY), -1.0)
    spectrum = lax.all_to_all(spectrum, "gx", split_axis=1, concat_axis=2, tiled=True)
    spectrum = complex_section(spectrum, forward_x, 2)
    spectrum = lax.all_to_all(spectrum, "gy", split_axis=2, concat_axis=3, tiled=True)
    spectrum = complex_section(spectrum, forward_y, 3)
    spectrum = lax.all_to_all(spectrum, "gx", split_axis=3, concat_axis=1, tiled=True)
    return spectrum


def to_cells(spectrum, width_x, width_y):
    backward_x = back_pair(width_x, signed_modes(KX))
    backward_y = back_pair(width_y, signed_modes(KY))
    spectrum = lax.all_to_all(spectrum, "gx", split_axis=1, concat_axis=3, tiled=True)
    spectrum = complex_section(spectrum, backward_y, 3)
    spectrum = lax.all_to_all(spectrum, "gy", split_axis=3, concat_axis=2, tiled=True)
    spectrum = complex_section(spectrum, backward_x, 2)
    spectrum = lax.all_to_all(spectrum, "gx", split_axis=2, concat_axis=1, tiled=True)
    cosine, sine_part = back_pair(NZ, jnp.arange(KZ, dtype=jnp.int32))
    return along(spectrum[0], cosine, 3) - along(spectrum[1], sine_part, 3)


def mix_modes(spectrum, weights):

    def product_part(spectra_in, weights_in):
        return jnp.einsum("cabk,abkco->oabk", spectra_in, weights_in, precision=precise)

    return jnp.stack(
        [
            product_part(spectrum[0], weights[0]) - product_part(spectrum[1], weights[1]),
            product_part(spectrum[1], weights[0]) + product_part(spectrum[0], weights[1]),
        ]
    )


def mix_adjoint(back_mixed, weights):

    def product_part(spectra_in, weights_in):
        return jnp.einsum("oabk,abkco->cabk", spectra_in, weights_in, precision=precise)

    return jnp.stack(
        [
            product_part(back_mixed[0], weights[0]) + product_part(back_mixed[1], weights[1]),
            product_part(back_mixed[1], weights[0]) - product_part(back_mixed[0], weights[1]),
        ]
    )


def weight_grad(spectrum, back_mixed):

    def product_part(spectra_in, backs_in):
        return jnp.einsum("cabk,oabk->abkco", spectra_in, backs_in, precision=precise)

    return jnp.stack(
        [
            product_part(spectrum[0], back_mixed[0]) + product_part(spectrum[1], back_mixed[1]),
            product_part(spectrum[0], back_mixed[1]) - product_part(spectrum[1], back_mixed[0]),
        ]
    )


def erf_gelu(values):
    return 0.5 * values * (1.0 + lax.erf(values * root_half))


def gelu_slope(values):
    return (
        0.5 * (1.0 + lax.erf(values * root_half))
        + values * jnp.exp(-0.5 * values * values) * inverse_root_two_pi
    )


def pointwise(grid_slab, spectral, expand_weight, reduce_weight, cotangent_slab):
    joined = (spectral + grid_slab.astype(jnp.float32)).astype(jnp.bfloat16)
    before = lax.dot_general(
        expand_weight, joined, (((0,), (0,)), ((), ())), preferred_element_type=jnp.float32
    )
    hidden = erf_gelu(before).astype(jnp.bfloat16)
    output = lax.dot_general(
        reduce_weight, hidden, (((0,), (0,)), ((), ())), preferred_element_type=jnp.float32
    )
    back_hidden = jnp.dot(reduce_weight, cotangent_slab, preferred_element_type=jnp.float32)
    back_before = (back_hidden * gelu_slope(before)).astype(jnp.bfloat16)
    grad_reduce = lax.dot_general(
        hidden, cotangent_slab, (((1,), (1,)), ((), ())), preferred_element_type=jnp.float32
    )
    grad_expand = lax.dot_general(
        joined, back_before, (((1,), (1,)), ((), ())), preferred_element_type=jnp.float32
    )
    back_joined = jnp.dot(expand_weight, back_before, preferred_element_type=jnp.float32)
    return (output.astype(jnp.bfloat16), back_joined, grad_expand, grad_reduce)


def local(grid_input, spectral_weight, expand_weight, reduce_weight, out_cotangent):
    channels, rows_x, merged = grid_input.shape
    rows_y = merged // NZ
    cell_count = rows_x * merged
    width_x = rows_x * lax.axis_size("gx")
    width_y = rows_y * lax.axis_size("gy")
    mode_scale = 1.0 / math.sqrt(width_x * width_y * NZ * KX * KY * (4 * KZ - 3))
    doubling = jnp.where(jnp.arange(KZ) == 0, 1.0, 2.0).astype(jnp.float32) * mode_scale
    spectrum = to_modes(
        grid_input.astype(jnp.float32).reshape(channels, rows_x, rows_y, NZ), width_x, width_y
    )
    weights = spectral_weight.astype(jnp.float32).reshape(
        2, spectral_weight.shape[1], spectral_weight.shape[2], KZ, channels, channels
    )
    mixed_modes = mix_modes(spectrum, weights) * doubling
    spectral = to_cells(mixed_modes, width_x, width_y).reshape(channels, cell_count)
    layer_output, back_joined, grad_expand, grad_reduce = pointwise(
        grid_input.reshape(channels, cell_count),
        spectral,
        expand_weight,
        reduce_weight,
        out_cotangent.reshape(channels, cell_count),
    )
    back_mixed = (
        to_modes(back_joined.reshape(channels, rows_x, rows_y, NZ), width_x, width_y) * doubling
    )
    grad_spectral = weight_grad(spectrum, back_mixed).reshape(spectral_weight.shape)
    back_modes = mix_adjoint(back_mixed, weights)
    back_cells = to_cells(back_modes, width_x, width_y).reshape(channels, cell_count)
    grad_input = (back_joined + back_cells).astype(jnp.bfloat16)
    grad_expand, grad_reduce = lax.psum((grad_expand, grad_reduce), ("gx", "gy"))
    rms_scale = 1.0 / math.sqrt(width_x * width_y * NZ)
    return (
        layer_output.reshape(channels, rows_x, merged),
        grad_input.reshape(channels, rows_x, merged),
        grad_spectral,
        grad_expand * rms_scale,
        grad_reduce * rms_scale,
    )


F32 = jnp.float32
BF16 = jnp.bfloat16
CH = 32
MESH = pl.DeviceIdType.MESH


def fits(mesh):
    return mesh.shape["gx"] * mesh.shape["gy"] == CH


def halves(matrix):
    high = matrix.astype(np.float32).astype(ml_dtypes.bfloat16)
    low = (matrix - high.astype(np.float64)).astype(np.float32).astype(ml_dtypes.bfloat16)
    return high, low


def embed(factor):
    return np.block([[factor.real, factor.imag], [-factor.imag, factor.real]])


def tables(count_x, count_y, rows_x, rows_y):
    width_x, width_y = count_x * rows_x, count_y * rows_y
    per_y = KY // count_x
    freq_x = np.where(np.arange(KX) < KX // 2, np.arange(KX), np.arange(KX) - KX)
    freq_y = np.where(np.arange(KY) < KY // 2, np.arange(KY), np.arange(KY) - KY)

    def angle(length, freq):
        return (np.arange(length)[:, None] * freq[None, :] % length) * (2.0 * np.pi / length)

    turn_x, turn_y = angle(width_x, freq_x), angle(width_y, freq_y)
    turn_z = angle(NZ, np.arange(KZ))
    z_pair = np.stack([np.cos(turn_z), -np.sin(turn_z)], axis=2)
    z_full = np.einsum("zlr,yw->yzlrw", z_pair, np.eye(rows_y)).reshape(rows_y * NZ, KZ * 2 * rows_y)
    z_back = z_full.T
    x_front = np.concatenate([np.cos(turn_x).T, np.sin(turn_x).T], axis=0)
    x_back = x_front.T
    wave = np.exp(-1j * turn_y)

    def y_matrix(factor):
        pair = embed(factor).reshape(2, count_y, rows_y, 2, count_x, per_y)
        full = np.einsum("rgysxk,lm->glryxskm", pair, np.eye(KZ))
        return full.reshape(count_y * KZ * 2 * rows_y, count_x * 2 * per_y * KZ)

    y_front = np.concatenate([y_matrix(wave), y_matrix(-1j * wave)], axis=0)
    y_back = np.concatenate([y_matrix(wave).T, y_matrix(-1j * wave).T], axis=1)
    eye = np.eye(CH)
    spread_c = np.repeat(eye, CH, axis=1)
    spread_o = np.tile(eye, (1, CH))
    scale = 1.0 / math.sqrt(width_x * width_y * NZ * KX * KY * (4 * KZ - 3))
    doubling = np.where(np.arange(KZ) == 0, 1.0, 2.0) * scale
    lanes = np.tile(doubling, 2 * per_y)[None, :].astype(np.float32)
    exact = ml_dtypes.bfloat16
    return (
        *halves(z_full), *halves(z_back), *halves(x_front), *halves(x_back),
        *halves(y_front), *halves(y_back),
        np.concatenate([spread_c] * 2, axis=0).astype(exact),
        np.concatenate([spread_o] * 2, axis=0).astype(exact),
        np.tile(eye, (1, 128 // CH)).astype(exact),
        spread_c.astype(exact),
        lanes,
    )


def split(values):
    high = values.astype(BF16)
    return high, (values - high.astype(F32)).astype(BF16)


def mm(left, right, dims=((1,), (0,))):
    return lax.dot_general(left, right, (dims, ((), ())), preferred_element_type=F32)


def right_table(values, high, low):
    rows = values.shape[0]
    value_high, value_low = split(values)
    both = mm(jnp.concatenate([value_high, value_low], axis=0), high)
    return both[:rows] + both[rows:] + mm(value_high, low)


def left_table(high, low, values):
    rows = high.shape[0]
    value_high, value_low = split(values)
    both = mm(jnp.concatenate([high, low], axis=0), value_high)
    return both[:rows] + both[rows:] + mm(high, value_low)


def kernel(
    count_x, count_y, rms_scale,
    u_ref, w_ref, ex_ref, ext_ref, re_ref, ret_ref, cot_ref,
    zfh, zfl, zbh, zbl, xfh, xfl, xbh, xbl, yfh, yfl, ybh, ybl,
    spread_c, spread_o, fold_c, fold_o, lanes,
    out_ref, gin_ref, gspec_ref, gex_ref, gre_ref,
    s1, r1, s2, r2, s3, r3, s4, r4, s5, r5, s6, r6, s7, r7, s8, r8,
    sg, rg, sh, rh,
    joined_buf, cot_buf, out_buf, bj_buf, modes_buf, bh_buf,
    send_sem, recv_sem,
):
    devices = count_x * count_y
    per_y = KY // count_x
    at_x, at_y = lax.axis_index("gx"), lax.axis_index("gy")
    at_group = lax.axis_index("groups")
    me = at_x * count_y + at_y
    my_turned = at_y * count_x + at_x
    rows_x = u_ref.shape[1]

    def peer(step):
        to = lax.rem(me + step, devices)
        return to, lax.div(to, count_y), lax.rem(to, count_y)

    barrier = pltpu.get_barrier_semaphore()

    def greet(step, carry):
        _, to_x, to_y = peer(step)
        pl.semaphore_signal(barrier, inc=1, device_id=(at_group, to_x, to_y), device_id_type=MESH)
        return carry

    lax.fori_loop(1, devices, greet, 0)

    def start(turn, source, target, turn_source, turn_target):
        def send(step, carry):
            to, to_x, to_y = peer(step)
            source_at = to_y * count_x + to_x if turn_source else to
            pltpu.make_async_remote_copy(
                src_ref=source.at[source_at],
                dst_ref=target.at[my_turned if turn_target else me],
                send_sem=send_sem.at[turn],
                recv_sem=recv_sem.at[turn],
                device_id=(at_group, to_x, to_y),
                device_id_type=MESH,
            ).start()
            return carry

        lax.fori_loop(1, devices, send, 0)
        target[my_turned if turn_target else me] = source[my_turned if turn_source else me]

    def finish(turn, source, target):
        copy = pltpu.make_async_remote_copy(
            src_ref=source.at[pl.ds(0, devices - 1)],
            dst_ref=target.at[pl.ds(0, devices - 1)],
            send_sem=send_sem.at[turn],
            recv_sem=recv_sem.at[turn],
            device_id=(at_group, at_x, at_y),
            device_id_type=MESH,
        )
        copy.wait_send()
        copy.wait_recv()

    def plane_modes(received, outgoing):
        planes = received[...].reshape(count_y, count_x * rows_x, 128)
        wide = jnp.concatenate([planes[g] for g in range(count_y)], axis=1)
        turned = left_table(xfh[...], xfl[...], wide)
        stacked = jnp.concatenate([turned[:KX], turned[KX:]], axis=1)
        modes = right_table(stacked, yfh[...], yfl[...])
        width = 2 * per_y * KZ
        for g in range(count_x):
            outgoing[pl.ds(g * count_y, count_y)] = modes[:, g * width:(g + 1) * width].reshape(
                count_y, KX // count_y, width
            )

    def plane_cells(received, outgoing):
        width = 2 * per_y * KZ
        blocks = received[...].reshape(count_x, KX, width)
        wide = jnp.concatenate([blocks[g] for g in range(count_x)], axis=1)
        both = right_table(wide, ybh[...], ybl[...])
        half = both.shape[1] // 2
        stacked = jnp.concatenate([both[:, :half], both[:, half:]], axis=0)
        cells = left_table(xbh[...], xbl[...], stacked)
        for g in range(count_y):
            outgoing[pl.ds(g * count_x, count_x)] = cells[:, g * 128:(g + 1) * 128].reshape(
                count_x, rows_x, 128
            )

    def spread(received, at, table):
        high, low = split(received[:, at, :])
        return mm(jnp.concatenate([high, low], axis=0), table, ((0,), (0,)))

    def weights_at(part, at):
        return w_ref[part, at].astype(F32).reshape(per_y * KZ, CH * CH)

    rows = CH * rows_x
    grid = u_ref[...].astype(F32).reshape(rows, u_ref.shape[2])
    grid_low = grid.astype(BF16)
    s1[...] = (mm(grid_low, zfh[...]) + mm(grid_low, zfl[...])).reshape(s1.shape)
    pl.semaphore_wait(barrier, devices - 1)
    start(0, s1, r1, False, True)
    cot_buf[...] = cot_ref[...].astype(F32)
    for at in range(rows_x):
        bh_buf[at] = mm(re_ref[...], cot_buf[:, at, :].astype(BF16))
    finish(0, s1, r1)
    plane_modes(r1, s2)
    start(1, s2, r2, False, False)
    finish(1, s2, r2)
    per_x = KX // count_y
    half = per_y * KZ
    for at in range(per_x):
        modes = spread(r2, at, spread_c[...])
        modes_buf[at] = modes
        real, imag = modes[:half], modes[half:]
        w_real, w_imag = weights_at(0, at), weights_at(1, at)
        mixed = jnp.concatenate(
            [real * w_real - imag * w_imag, imag * w_real + real * w_imag], axis=0
        )
        total = mixed[:, :128]
        for g in range(1, CH * CH // 128):
            total = total + mixed[:, g * 128:(g + 1) * 128]
        high, low = split(total)
        fold = fold_c[...]
        s3[:, at, :] = (mm(fold, high, ((1,), (1,))) + mm(fold, low, ((1,), (1,)))) * lanes[...]
    start(2, s3, r3, False, False)
    finish(2, s3, r3)
    plane_cells(r3, s4)
    start(3, s4, r4, True, False)
    finish(3, s4, r4)
    spectral = right_table(r4[...].reshape(rows, 128), zbh[...], zbl[...])
    joined_buf[...] = (spectral + u_ref[...].astype(F32).reshape(rows, u_ref.shape[2])).reshape(
        joined_buf.shape
    )
    grad_expand = jnp.zeros((CH, ex_ref.shape[1]), F32)
    grad_reduce = jnp.zeros((CH, ex_ref.shape[1]), F32)
    for at in range(rows_x):
        joined = joined_buf[:, at, :].astype(BF16)
        cotangent = cot_buf[:, at, :].astype(BF16)
        before = mm(ext_ref[...], joined)
        below = 0.5 * (1.0 + lax.erf(before * root_half))
        hidden = (before * below).astype(BF16)
        slope = below + before * jnp.exp(-0.5 * before * before) * inverse_root_two_pi
        back_before = (bh_buf[at] * slope).astype(BF16)
        out_buf[:, at, :] = mm(ret_ref[...], hidden)
        grad_reduce = grad_reduce + mm(cotangent, hidden, ((1,), (1,)))
        grad_expand = grad_expand + mm(joined, back_before, ((1,), (1,)))
        bj_buf[:, at, :] = mm(ex_ref[...], back_before)
    s5[...] = right_table(bj_buf[...].reshape(rows, u_ref.shape[2]), zfh[...], zfl[...]).reshape(
        s5.shape
    )
    start(4, s5, r5, False, True)
    sg[:, 0, :] = grad_expand
    sg[:, 1, :] = grad_reduce
    start(8, sg, rg, False, False)
    out_ref[...] = out_buf[...].astype(BF16)
    finish(4, s5, r5)
    plane_modes(r5, s6)
    start(5, s6, r6, False, False)
    finish(8, sg, rg)
    total = jnp.sum(rg[...], axis=0) * rms_scale
    sh[...] = jnp.broadcast_to(total[None], sh.shape)
    start(9, sh, rh, False, False)
    finish(5, s6, r6)
    for at in range(per_x):
        back = spread(r6, at, spread_o[...])
        real, imag = back[:half], back[half:]
        w_real, w_imag = weights_at(0, at), weights_at(1, at)
        mixed = jnp.concatenate(
            [real * w_real + imag * w_imag, imag * w_real - real * w_imag], axis=0
        )
        high, low = split(mixed)
        fold = fold_o[...]
        s7[:, at, :] = (mm(fold, high, ((1,), (1,))) + mm(fold, low, ((1,), (1,)))) * lanes[...]
    start(6, s7, r7, False, False)
    scale_rows = (lax.broadcasted_iota(jnp.int32, (half, 128), 0) % KZ == 0)
    unit = 1.0 / math.sqrt(
        count_x * rows_x * count_y * (u_ref.shape[2] // NZ) * NZ * KX * KY * (4 * KZ - 3)
    )
    scale = jnp.where(scale_rows, unit, 2.0 * unit)[:, :1]
    for at in range(per_x):
        back = spread(r6, at, spread_o[...])
        back_real, back_imag = back[:half] * scale, back[half:] * scale
        modes = modes_buf[at]
        real, imag = modes[:half], modes[half:]
        shape = gspec_ref.shape[2:]
        gspec_ref[0, at] = (real * back_real + imag * back_imag).reshape(shape)
        gspec_ref[1, at] = (real * back_imag - imag * back_real).reshape(shape)
    finish(6, s7, r7)
    plane_cells(r7, s8)
    start(7, s8, r8, True, False)
    finish(9, sh, rh)
    gex_ref[...] = rh[:, 0, :]
    gre_ref[...] = rh[:, 1, :].T
    finish(7, s8, r8)
    cells = right_table(r8[...].reshape(rows, 128), zbh[...], zbl[...])
    gin_ref[...] = (bj_buf[...] + cells.reshape(bj_buf.shape)).astype(BF16)


def fused(grid_input, spectral_weight, expand_weight, reduce_weight, out_cotangent):
    channels, rows_x, merged = grid_input.shape
    rows_y = merged // NZ
    count_x, count_y = lax.axis_size("gx"), lax.axis_size("gy")
    hidden_units = expand_weight.shape[1]
    per_x, per_y = KX // count_y, KY // count_x
    constants = tables(count_x, count_y, rows_x, rows_y)
    rms_scale = 1.0 / math.sqrt(count_x * rows_x * count_y * rows_y * NZ)
    operands = (
        grid_input, spectral_weight, expand_weight, expand_weight.T, reduce_weight,
        reduce_weight.T, out_cotangent, *[jnp.asarray(table) for table in constants],
    )
    tile = pltpu.VMEM((CH, rows_x, 2 * KZ * rows_y), F32)
    freq = pltpu.VMEM((CH, per_x, 2 * per_y * KZ), F32)
    pair = pltpu.VMEM((CH, 2, hidden_units), F32)
    field = pltpu.VMEM(grid_input.shape, F32)
    half_round = [tile, tile, freq, freq, freq, freq, tile, tile]
    vmem = pl.BlockSpec(memory_space=pltpu.VMEM)
    call = pl.pallas_call(
        lambda *refs: kernel(count_x, count_y, rms_scale, *refs),
        out_shape=(
            jax.ShapeDtypeStruct(grid_input.shape, BF16),
            jax.ShapeDtypeStruct(grid_input.shape, BF16),
            jax.ShapeDtypeStruct(spectral_weight.shape, F32),
            jax.ShapeDtypeStruct((CH, hidden_units), F32),
            jax.ShapeDtypeStruct((hidden_units, CH), F32),
        ),
        in_specs=[vmem] * len(operands),
        out_specs=(vmem,) * 5,
        scratch_shapes=[
            *half_round, *half_round, pair, pair, pair, pair,
            field, field, field, field,
            pltpu.VMEM((per_x, 2 * per_y * KZ, CH * CH), F32),
            pltpu.VMEM((rows_x, hidden_units, merged), F32),
            pltpu.SemaphoreType.DMA((10,)),
            pltpu.SemaphoreType.DMA((10,)),
        ],
        compiler_params=pltpu.CompilerParams(
            collective_id=0, has_side_effects=True, vmem_limit_bytes=56 * 1024 * 1024
        ),
    )
    return call(*operands)


def solution(mesh):
    in_specs = (
        P("groups", "gx", "gy"),
        P(None, "gy", "gx", None, None),
        P(),
        P(),
        P("groups", "gx", "gy"),
    )
    out_specs = (
        P("groups", "gx", "gy"),
        P("groups", "gx", "gy"),
        P("groups", "gy", "gx", None, None),
        P("groups", None),
        P("groups", None),
    )
    return jax.shard_map(fused if fits(mesh) else local, mesh=mesh, in_specs=in_specs, out_specs=out_specs, check_vma=False)
```
